32 devices in a mesh: ens: 2 (over y), gx: 4 (over z), ta: 2 (over x), col: 2 (over core).
Axes of the slice: x: 2, y: 2, z: 4, core: 2. Of those that a mesh axis runs over, the one named last changes fastest.
Arguments:
- frames: bfloat16 [40, 4, 128, 128, 128], P('ens', 'ta', 'gx', 'col'), parts along dimension 0, may hold values from -6 to 6
- counts: int32 [8], P('ens'), parts along dimension 0, may hold values from 1 to 3
- spectral_weight: bfloat16 [2, 40, 20, 65536], P(None, 'ens', 'col', 'gx'), parts along dimension 1, may hold values from -6 to 6
- point_weight: bfloat16 [40, 20], P('ens'), parts along dimension 0, may hold values from -1.25 to 1.25
- point_bias: float32 [40], P('ens'), parts along dimension 0, may hold values from -3 to 3
Outputs:
- layer_out: bfloat16 [40, 4, 128, 128, 128], P('ens', 'ta', 'gx', 'col'), parts along dimension 0
The draws below stay inside these ranges and needn't reach their ends.
There are 2 independent parts, one for each index of `ens`. The reference program is written for one: setup_inputs(seed, part) draws one part's arguments, and reference() takes and returns one part's arrays. A program takes and returns all parts, laid end to end along the dimension named above; each array names one. Nothing has to cross between parts.
All inputs are finite; a program needn't handle non-finite values.
Results may differ from the reference program's by a relative error of at most 0.0029.
Values may be sent and summed in bfloat16 or wider, within the bound.
A program may use at most 384 MiB of HBM per device.

```python
import math
import jax
import jax.numpy as jnp
from jax import lax

C = 20
T_SIZE = 4
X = 128
Y = 128
Z = 128
MX = 32
MY = 32
MZ = 32
MT = 2
MODES = 65536


def place_ends(entries, rng, smallest, high):
    place = [jax.random.randint(jax.random.fold_in(rng, axis), (), 0, length) for axis, length in enumerate(entries.shape)]
    widest = entries.shape.index(max(entries.shape))
    next_to = place[:widest] + [(place[widest] + 1) % entries.shape[widest]] + place[widest + 1:]
    return entries.at[tuple(place)].set(smallest).at[tuple(next_to)].set(high)


def block_levels(rng, shape, shards, least, top_value):
    def one(position, parts):
        heights = jax.random.uniform(jax.random.fold_in(jax.random.fold_in(rng, 6), position), (parts,), jnp.float32, least / len(shards), top_value / len(shards))
        return jnp.repeat(jnp.exp(heights), shape[position] // parts).reshape((-1,) + (1,) * (len(shape) - position - 1))

    gain = one(*shards[0])
    for cut in shards[1:]:
        gain = gain * one(*cut)
    return gain


def bell_draw(key, shape, width, reach, shards=(), kind=jnp.bfloat16):
    values = width * jax.random.normal(key, shape, jnp.float32)
    if shards:
        values = values * block_levels(key, shape, shards, -0.22, 0.18)
    return jnp.clip(values, -reach, reach).astype(kind)


def setup_inputs(seed: int = 0, part: int = 0) -> dict:
    key_list = jax.random.split(jax.random.key(seed), 6)
    part_splits = jax.random.split(jax.random.fold_in(key_list[5], part), 6)
    return {
        "frames": bell_draw(part_splits[0], (C, T_SIZE, X, Y, Z), 1.0, 6.0, ((1, 2), (2, 4), (3, 2))),
        "counts": place_ends(jax.random.randint(part_splits[1], (T_SIZE,), 1, 4), jax.random.fold_in(part_splits[1], 1), 1, 3).astype(jnp.int32),
        "spectral_weight": bell_draw(part_splits[2], (2, C, C, MODES), 1.0, 6.0, ((2, 2), (3, 4))),
        "point_weight": bell_draw(part_splits[3], (C, C), C ** -0.5, 1.25),
        "point_bias": bell_draw(part_splits[4], (C,), 0.5, 3.0, (), jnp.float32),
    }


def centered_modes(mode_count):
    places = jnp.arange(mode_count, dtype=jnp.int32)
    return jnp.where(places < mode_count // 2, places, places - mode_count)


def phase_table(points, frequencies, length):
    product = jnp.remainder(points[:, None] * frequencies[None, :], length)
    return product.astype(jnp.float32) * (2.0 * math.pi / length)


def reference(frames, counts, spectral_weight, point_weight, point_bias):
    highest = lax.Precision.HIGHEST
    pencil_count = MY * MZ
    y_angles = phase_table(jnp.arange(Y, dtype=jnp.int32), centered_modes(MY), Y)
    ytable = jnp.concatenate([jnp.cos(y_angles), -jnp.sin(y_angles)], axis=1).astype(jnp.bfloat16)
    z_angles = phase_table(jnp.arange(Z, dtype=jnp.int32), jnp.arange(MZ, dtype=jnp.int32), Z)
    z_table = jnp.concatenate([jnp.cos(z_angles), jnp.sin(z_angles)], axis=1)
    x_angles = phase_table(jnp.arange(X, dtype=jnp.int32), centered_modes(MX), X)
    x_cos = jnp.cos(x_angles)
    x_sin = jnp.sin(x_angles)
    t_angles = phase_table(jnp.arange(T_SIZE, dtype=jnp.int32), jnp.arange(MT, dtype=jnp.int32), T_SIZE)
    time_cos = jnp.cos(t_angles)
    time_sin = jnp.sin(t_angles)
    frame_scale = counts.astype(jnp.float32)

    def forward_frame(step_index):
        frame = lax.dynamic_index_in_dim(frames, step_index, 1, keepdims=False)
        first = jnp.einsum('cxyz,yj->cxjz', frame.astype(jnp.float32), ytable.astype(jnp.float32), precision=highest)
        second = jnp.einsum('cxjz,zk->cxjk', first, z_table, precision=highest)
        real_part = (second[:, :, :MY, :MZ] + second[:, :, MY:, MZ:]).reshape(C, X, pencil_count)
        imag_part = (second[:, :, MY:, :MZ] - second[:, :, :MY, MZ:]).reshape(C, X, pencil_count)
        real_x = jnp.einsum('cxp,xk->ckp', real_part, x_cos, precision=highest) + jnp.einsum('cxp,xk->ckp', imag_part, x_sin, precision=highest)
        imag_x = jnp.einsum('cxp,xk->ckp', imag_part, x_cos, precision=highest) - jnp.einsum('cxp,xk->ckp', real_part, x_sin, precision=highest)
        return jnp.stack([real_x, imag_x]) * frame_scale[step_index]

    spectra = lax.map(forward_frame, jnp.arange(T_SIZE, dtype=jnp.int32))
    real_t = jnp.einsum('tckp,tm->cmkp', spectra[:, 0], time_cos, precision=highest) + jnp.einsum('tckp,tm->cmkp', spectra[:, 1], time_sin, precision=highest)
    imag_t = jnp.einsum('tckp,tm->cmkp', spectra[:, 1], time_cos, precision=highest) - jnp.einsum('tckp,tm->cmkp', spectra[:, 0], time_sin, precision=highest)
    mixing = spectral_weight.astype(jnp.float32).reshape(2, C, C, pencil_count, MT, MX)
    real_v = jnp.einsum('oipmk,imkp->omkp', mixing[0], real_t, precision=highest) - jnp.einsum('oipmk,imkp->omkp', mixing[1], imag_t, precision=highest)
    imag_v = jnp.einsum('oipmk,imkp->omkp', mixing[0], imag_t, precision=highest) + jnp.einsum('oipmk,imkp->omkp', mixing[1], real_t, precision=highest)

    z_weight = jnp.where(jnp.arange(MZ, dtype=jnp.int32) == 0, 1.0, 2.0).astype(jnp.float32) / float(T_SIZE * X * Y * Z)
    z_cos_inv = jnp.cos(z_angles).T * z_weight[:, None]
    z_sin_inv = jnp.sin(z_angles).T * z_weight[:, None]
    y_inverse = jnp.concatenate([jnp.cos(y_angles).T, -jnp.sin(y_angles).T], axis=0)
    weight_full = point_weight.astype(jnp.float32)

    def inverse_frame(step_index):
        t_cos = time_cos[step_index]
        t_sin = time_sin[step_index]
        g_real = jnp.einsum('omkp,m->okp', real_v, t_cos, precision=highest) - jnp.einsum('omkp,m->okp', imag_v, t_sin, precision=highest)
        g_imag = jnp.einsum('omkp,m->okp', imag_v, t_cos, precision=highest) + jnp.einsum('omkp,m->okp', real_v, t_sin, precision=highest)
        h_real = jnp.einsum('okp,xk->oxp', g_real, x_cos, precision=highest) - jnp.einsum('okp,xk->oxp', g_imag, x_sin, precision=highest)
        h_imag = jnp.einsum('okp,xk->oxp', g_imag, x_cos, precision=highest) + jnp.einsum('okp,xk->oxp', g_real, x_sin, precision=highest)
        h_real = h_real.reshape(C, X, MY, MZ)
        h_imag = h_imag.reshape(C, X, MY, MZ)
        z_real = jnp.einsum('oxjk,kz->oxjz', h_real, z_cos_inv, precision=highest) - jnp.einsum('oxjk,kz->oxjz', h_imag, z_sin_inv, precision=highest)
        z_imag = jnp.einsum('oxjk,kz->oxjz', h_imag, z_cos_inv, precision=highest) + jnp.einsum('oxjk,kz->oxjz', h_real, z_sin_inv, precision=highest)
        stacked = jnp.concatenate([z_real, z_imag], axis=2)
        spectral = jnp.einsum('oxjz,jy->oxyz', stacked, y_inverse, precision=highest)
        frame = lax.dynamic_index_in_dim(frames, step_index, 1, keepdims=False)
        pointwise = jnp.einsum('oi,ixyz->oxyz', weight_full, frame.astype(jnp.float32), precision=highest) * frame_scale[step_index]
        summed = spectral + pointwise + point_bias[:, None, None, None]
        return jax.nn.gelu(summed).astype(jnp.bfloat16)

    outputs = lax.map(inverse_frame, jnp.arange(T_SIZE, dtype=jnp.int32))
    return jnp.moveaxis(outputs, 0, 1)
```

```python
import functools

import jax
import jax.numpy as jnp
import numpy as np
from jax import lax
from jax.experimental import pallas as pl
from jax.experimental.pallas import tpu as pltpu
from jax.sharding import PartitionSpec as P

MX = 32
MY = 32
MZ = 32
MT = 2
PACK = 4
F32 = jnp.float32
BF16 = jnp.bfloat16


def centered(count):
    places = np.arange(count)
    return np.where(places < count // 2, places, places - count)


def angles(points, frequencies, length):
    return (np.outer(points, frequencies) % length) * (2.0 * np.pi / length)


def split(value):
    high = value.astype(BF16)
    return high, (value - high.astype(F32)).astype(BF16)


def dot(a, b):
    return jnp.dot(a, b, preferred_element_type=F32)


def forward_kernel(steps, rows_y, f_ref, z_ref, y_ref, x_ref, out_ref, held):
    at_once = 4 if steps % 4 == 0 else 1

    def cells(block, carry):
        base = block * at_once
        wide = jnp.concatenate(
            [
                f_ref[c, 0, pl.ds(base, at_once)].reshape(at_once * rows_y, f_ref.shape[-1])
                for c in range(PACK)
            ],
            axis=1,
        )
        g = dot(wide, z_ref[0]) + dot(wide, z_ref[1])
        for s in range(at_once):
            part = g[s * rows_y : (s + 1) * rows_y]
            pair = jnp.concatenate([part[:, : PACK * MZ], part[:, PACK * MZ :]], axis=0)
            high, low = split(pair)
            held[pl.ds(pl.multiple_of((base + s) * 2 * MY, 2 * MY), 2 * MY), :] = dot(
                y_ref[...], jnp.concatenate([high, low], axis=0)
            )
        return carry

    lax.fori_loop(0, steps // at_once, cells, 0)
    half = PACK * MZ // 2
    lane = lax.broadcasted_iota(jnp.int32, (MT * MX, PACK * MZ), 1)

    def modes(ky, carry):
        real = held[pl.ds(ky, steps, stride=2 * MY), :]
        imag = held[pl.ds(ky + MY, steps, stride=2 * MY), :]
        high, low = split(jnp.concatenate([real, imag], axis=0))
        m = dot(x_ref[0], high) + dot(x_ref[0], low) + dot(x_ref[1], high)
        m_real, m_imag = m[: MT * MX], m[MT * MX :]
        out_ref[0, 0, ky] = jnp.where(lane < half, m_real, pltpu.roll(m_imag, half, 1))
        out_ref[1, 0, ky] = jnp.where(lane < half, pltpu.roll(m_real, half, 1), m_imag)
        return carry

    lax.fori_loop(0, MY, modes, 0, unroll=2)


def mixing_kernel(outputs, w_ref, m_ref, out_ref):
    m_real, m_imag = m_ref[0], m_ref[1]
    for o in range(outputs):
        w_real = w_ref[0, o].astype(F32)
        w_imag = w_ref[1, o].astype(F32)
        out_ref[0, pl.ds(o, 1), :] = jnp.sum(
            w_real * m_real - w_imag * m_imag, axis=0, keepdims=True
        )
        out_ref[1, pl.ds(o, 1), :] = jnp.sum(
            w_real * m_imag + w_imag * m_real, axis=0, keepdims=True
        )


def inverse_kernel(
    steps, groups, rows_y, m_ref, f_ref, x_ref, y_ref, z_ref, p_ref, c_ref, b_ref, out_ref, held, spec
):
    half = PACK * MZ // 2
    parts, kys = m_ref.shape[0], m_ref.shape[3]
    x_block = f_ref.shape[2]
    z_cells = f_ref.shape[4]
    channels = groups * PACK
    t_now, x_now = pl.program_id(0), pl.program_id(1)

    @pl.when(jnp.logical_and(t_now == 0, x_now == 0))
    def _():
        lane = lax.broadcasted_iota(jnp.int32, (MT * MX, PACK * MZ), 1)

        def one(index, carry):
            part = index // kys
            k = index % kys
            ky = index
            for g in range(groups):
                first = m_ref[part, 0, g, k].astype(F32)
                second = m_ref[part, 1, g, k].astype(F32)
                real = jnp.where(lane < half, first, pltpu.roll(second, half, 1))
                imag = jnp.where(lane < half, pltpu.roll(first, half, 1), second)
                high, low = split(jnp.concatenate([real, imag], axis=0))
                h = dot(x_ref[0], high) + dot(x_ref[0], low) + dot(x_ref[1], high)
                held[g, pl.ds(ky * steps, steps), :] = h[:steps]
                held[g, pl.ds((ky + MY) * steps, steps), :] = h[steps:]
            return carry

        lax.fori_loop(0, parts * kys, one, 0)

    scale = c_ref[t_now]

    def cell(x, carry):
        tx = (t_now * pl.num_programs(1) + x_now) * x_block + x
        for g in range(groups):
            high, low = split(held[g, pl.ds(tx, 2 * MY, stride=steps), :])
            d = dot(y_ref[0], high) + dot(y_ref[0], low) + dot(y_ref[1], high)
            wide = jnp.concatenate([d[:rows_y], d[rows_y:]], axis=1)
            high, low = split(wide)
            s = dot(high, z_ref[0]) + dot(low, z_ref[0]) + dot(high, z_ref[1])
            for u in range(PACK):
                spec[u * groups + g] = s[:, u * z_cells : (u + 1) * z_cells]
        for y in range(0, rows_y, 32):
            both = jnp.concatenate(
                [
                    f_ref[:, 0, x, y + 16 * s : y + 16 * (s + 1), :].reshape(channels * 16, z_cells)
                    for s in range(2)
                ],
                axis=1,
            )
            point = dot(p_ref[...], both) * scale
            for c in range(channels):
                for s in range(2):
                    low_y = y + 16 * s
                    v = (
                        spec[c, low_y : low_y + 16, :]
                        + point[c * 16 : (c + 1) * 16, s * z_cells : (s + 1) * z_cells]
                        + b_ref[c]
                    )
                    inner = v * (0.7978845608028654 + 0.035677408136300125 * (v * v))
                    hv = 0.5 * v
                    out_ref[c, 0, x, low_y : low_y + 16, :] = (hv + hv * jnp.tanh(inner)).astype(
                        out_ref.dtype
                    )
        return carry

    lax.fori_loop(0, x_block, cell, 0)


def per_device(sizes, frames, counts, spectral_weight, point_weight, point_bias):
    gx_size, ta_size, col_size = sizes
    channels, t_local, x_local, rows_y, z_cells = frames.shape
    t_size, x_size, y_size = t_local * ta_size, x_local * gx_size, rows_y * col_size
    groups = channels // PACK
    steps = t_local * x_local
    ky_share = MY // gx_size
    lanes = PACK * MZ
    col = lax.axis_index("col")
    ta = lax.axis_index("ta")
    gx = lax.axis_index("gx")
    vmem = 56 * 1024 * 1024

    z_ang = angles(np.arange(z_cells), np.arange(MZ), z_cells)
    eye = np.eye(PACK)
    z_fwd = np.concatenate([np.kron(eye, np.cos(z_ang)), np.kron(eye, np.sin(z_ang))], axis=1)
    z_fwd = jnp.stack(split(jnp.asarray(z_fwd, F32)))
    weight = np.where(np.arange(MZ) == 0, 1.0, 2.0)[:, None] / float(
        t_size * x_size * y_size * z_cells
    )
    z_inv = np.concatenate(
        [np.kron(eye, np.cos(z_ang).T * weight), np.kron(eye, -np.sin(z_ang).T * weight)], axis=0
    )
    z_inv = jnp.stack(split(jnp.asarray(z_inv, F32)))
    y_ang = angles(np.arange(y_size), centered(MY), y_size)
    y_cos, y_sin = np.cos(y_ang).T, np.sin(y_ang).T
    y_fwd = jnp.asarray(np.stack([np.stack([y_cos, -y_sin], 1), np.stack([-y_sin, -y_cos], 1)]), F32)
    y_fwd = lax.dynamic_slice_in_dim(y_fwd, col * rows_y, rows_y, 3).astype(BF16)
    y_fwd = y_fwd.reshape(2 * MY, 2 * rows_y)
    y_fwd = jnp.concatenate([y_fwd, y_fwd], axis=1)
    y_inv = jnp.asarray(
        np.stack([np.stack([y_cos.T, -y_sin.T], 1), np.stack([y_sin.T, y_cos.T], 1)]), F32
    )
    y_inv = lax.dynamic_slice_in_dim(y_inv, col * rows_y, rows_y, 1).reshape(2 * rows_y, 2 * MY)
    y_inv = jnp.stack(split(y_inv))
    x_ang = angles(np.arange(x_size), centered(MX), x_size).T
    t_ang = angles(np.arange(t_size), np.arange(MT), t_size).T
    tx_ang = t_ang[:, None, :, None] + x_ang[None, :, None, :]
    tx = jnp.asarray(np.stack([np.cos(tx_ang), np.sin(tx_ang)]), F32)
    tx = lax.dynamic_slice(
        tx,
        (0, 0, 0, ta * t_local, gx * x_local),
        (2, MT, MX, t_local, x_local),
    ).reshape(2, MT * MX, t_local, x_local)
    frame_scale = lax.dynamic_slice_in_dim(counts, ta * t_local, t_local).astype(F32)
    scaled = (tx * frame_scale[None, None, :, None]).reshape(2, MT * MX, steps)
    x_fwd = jnp.concatenate(
        [
            jnp.concatenate([scaled[0], scaled[1]], axis=1),
            jnp.concatenate([-scaled[1], scaled[0]], axis=1),
        ],
        axis=0,
    )
    x_fwd = jnp.stack(split(x_fwd))
    tx = tx.reshape(2, MT * MX, steps)
    x_inv = jnp.concatenate(
        [
            jnp.concatenate([tx[0].T, -tx[1].T], axis=1),
            jnp.concatenate([tx[1].T, tx[0].T], axis=1),
        ],
        axis=0,
    )
    x_inv = jnp.stack(split(x_inv))
    point_table = jnp.kron(point_weight.astype(F32), jnp.eye(16, dtype=F32)).astype(BF16)

    whole = lambda *shape: pl.BlockSpec(shape, lambda *_: (0,) * len(shape))
    partial = pl.pallas_call(
        functools.partial(forward_kernel, steps, rows_y),
        grid=(groups,),
        in_specs=[
            pl.BlockSpec((PACK, 1, steps, rows_y, z_cells), lambda g: (0, g, 0, 0, 0)),
            whole(*z_fwd.shape),
            whole(*y_fwd.shape),
            whole(*x_fwd.shape),
        ],
        out_specs=pl.BlockSpec((2, 1, MY, MT * MX, lanes), lambda g: (0, g, 0, 0, 0)),
        out_shape=jax.ShapeDtypeStruct((2, groups, MY, MT * MX, lanes), F32),
        scratch_shapes=[pltpu.VMEM((steps * 2 * MY, lanes), F32)],
        compiler_params=pltpu.CompilerParams(vmem_limit_bytes=vmem),
    )(frames.reshape(PACK, groups, steps, rows_y, z_cells), z_fwd, y_fwd, x_fwd)

    swap = [(0, 1), (1, 0)]
    mine = lax.dynamic_index_in_dim(partial, col, 0, keepdims=False)
    other = lax.dynamic_index_in_dim(partial, 1 - col, 0, keepdims=False)
    mine = (mine + lax.ppermute(other, "col", swap)).astype(BF16)
    mine = mine.reshape(groups, gx_size, ky_share, MT * MX, lanes).transpose(1, 0, 2, 3, 4)
    received = lax.all_to_all(mine, "gx", split_axis=0, concat_axis=0, tiled=True)
    modes = jnp.sum(received.astype(F32), axis=0)
    modes = lax.psum(modes, "ta")

    inputs = channels // 2
    flat = ky_share * MZ * MT * MX
    modes = modes.reshape(groups, ky_share, MT * MX, 2, 2, MZ).transpose(3, 4, 0, 1, 5, 2)
    modes = modes.reshape(2, inputs, flat)
    block = min(flat, 2048)
    mixed = pl.pallas_call(
        functools.partial(mixing_kernel, channels),
        grid=(flat // block,),
        in_specs=[
            pl.BlockSpec((2, channels, inputs, block), lambda q: (0, 0, 0, q)),
            pl.BlockSpec((2, inputs, block), lambda q: (0, 0, q)),
        ],
        out_specs=pl.BlockSpec((2, channels, block), lambda q: (0, 0, q)),
        out_shape=jax.ShapeDtypeStruct((2, channels, flat), F32),
        compiler_params=pltpu.CompilerParams(vmem_limit_bytes=vmem),
    )(spectral_weight, modes)

    mixed = mixed.reshape(2, 2, 2, groups, ky_share, MZ, MT * MX).transpose(1, 3, 4, 6, 0, 2, 5)
    mixed = mixed.reshape(2, groups, ky_share, MT * MX, lanes)
    mine = lax.dynamic_index_in_dim(mixed, col, 0, keepdims=False)
    other = lax.dynamic_index_in_dim(mixed, 1 - col, 0, keepdims=False)
    mine = mine + lax.ppermute(other, "col", swap)
    every = lax.all_gather(mine, ("gx", "col"), axis=0, tiled=False)
    every = every.reshape(gx_size, 2, groups, ky_share, MT * MX, lanes)

    x_block = min(x_local, 4)
    frame_spec = pl.BlockSpec(
        (channels, 1, x_block, rows_y, z_cells), lambda t, x: (0, t, x, 0, 0)
    )
    smem = pl.BlockSpec(memory_space=pltpu.SMEM)
    return pl.pallas_call(
        functools.partial(inverse_kernel, steps, groups, rows_y),
        grid=(t_local, x_local // x_block),
        in_specs=[
            pl.BlockSpec(every.shape, lambda t, x: (0,) * 6, pipeline_mode=pl.Buffered(1)),
            frame_spec,
            whole(*x_inv.shape),
            whole(*y_inv.shape),
            whole(*z_inv.shape),
            whole(*point_table.shape),
            smem,
            smem,
        ],
        out_specs=frame_spec,
        out_shape=jax.ShapeDtypeStruct(frames.shape, BF16),
        scratch_shapes=[
            pltpu.VMEM((groups, 2 * MY * steps, lanes), F32),
            pltpu.VMEM((channels, rows_y, z_cells), F32),
        ],
        compiler_params=pltpu.CompilerParams(vmem_limit_bytes=vmem),
    )(every, frames, x_inv, y_inv, z_inv, point_table, frame_scale, point_bias)


def solution(mesh):
    sizes = (mesh.shape["gx"], mesh.shape["ta"], mesh.shape["col"])
    return jax.shard_map(
        functools.partial(per_device, sizes),
        mesh=mesh,
        in_specs=(
            P("ens", "ta", "gx", "col", None),
            P("ens"),
            P(None, "ens", "col", "gx"),
            P("ens", None),
            P("ens"),
        ),
        out_specs=P("ens", "ta", "gx", "col", None),
        check_vma=False,
    )
```
